256 devices in a mesh: dp: 8 (over z_hi, core), tensor: 16 (over x, y), pipe: 2 (over z_lo).
Axes of the slice: x: 4, y: 4, z: 8 (z_hi: 4, z_lo: 2; z = z_hi * 2 + z_lo), core: 2. Of those that a mesh axis runs over, the one named last changes fastest.
Arguments:
- inputs: bfloat16 [2, 3072, 2304], P('pipe', 'dp'), may hold values from -8 to 8
- out_grad: bfloat16 [2, 3072, 2304], P('pipe', 'dp'), may hold values from -8 to 8
- gate_pre: bfloat16 [2, 3072, 18432], P('pipe', 'dp', 'tensor'), may hold values from -8 to 8
- up_pre: bfloat16 [2, 3072, 18432], P('pipe', 'dp', 'tensor'), may hold values from -8 to 8
- gate_weight: bfloat16 [2, 2304, 18432], P('pipe', 'dp', 'tensor'), may hold values from -0.125 to 0.125
- up_weight: bfloat16 [2, 2304, 18432], P('pipe', 'dp', 'tensor'), may hold values from -0.125 to 0.125
- down_weight: bfloat16 [2, 2304, 18432], P('pipe', 'dp', 'tensor'), may hold values from -0.046875 to 0.046875
- noise_gate: bfloat16 [2, 2304, 18432], P('pipe', 'dp', 'tensor'), may hold values from -768 to 768
- noise_up: bfloat16 [2, 2304, 18432], P('pipe', 'dp', 'tensor'), may hold values from -768 to 768
- noise_down: bfloat16 [2, 2304, 18432], P('pipe', 'dp', 'tensor'), may hold values from -768 to 768
- example_of_block: int32 [8, 3], P('dp'), may hold values from 0 to 1, never falling along the last dimension, each value on 1 to 2 neighbouring positions
- tail_tokens: int32 [16], P('dp'), may hold values from 1 to 128
Outputs:
- input_grad: bfloat16 [2, 3072, 2304], P('pipe', ('dp', 'tensor'))
- grad_gate: bfloat16 [2, 2304, 18432], P('pipe', 'dp', 'tensor')
- grad_up: bfloat16 [2, 2304, 18432], P('pipe', 'dp', 'tensor')
- grad_down: bfloat16 [2, 2304, 18432], P('pipe', 'dp', 'tensor')
- norm_ratio: float32 [16], P('dp')
The draws below stay inside these ranges and needn't reach their ends.
Inputs may be any that keep to these rules, and one draw needn't show every extreme that they name: `example_of_block`: row j gives, for each of the 3 blocks of 128 token slots of index j of dp, which of that index's 2 examples it belongs to; the numbers never fall along a row, every example has 1 to 2 whole blocks, and one example of each row has exactly 2.
All inputs are finite; a program needn't handle non-finite values.
Results may differ from the reference program's by a relative error of at most 0.018.
Values may be sent and summed in bfloat16 or wider, within the bound.
No kernel may reach another device: no remote copies, remote signals or barrier semaphores. Data moves between devices by JAX's collectives and lax.ppermute only.
A program may use at most 128 MiB of HBM per device.

```python
import math
import jax
import jax.numpy as jnp
import numpy as np
from jax import lax

D = 2304
FF = 18432
BLOCK = 128
TOK_DEV = 384
NB = 3
EX_DEV = 2
MOST_BLOCKS = 2
DP_GROUPS = 8
EXAMPLES = 16
TOKENS = 3072
LAYERS = 2
N_DP = 8
N_TENSOR = 16


def mixture_drawn(key, shape, col_shape):
    first, second = jax.random.split(key)
    column = jax.random.normal(first, col_shape, jnp.float32)
    spread = jax.random.normal(second, shape, jnp.float32)
    return 0.6 * column + 0.8 * spread


def draw_inputs(key, part):
    key = jax.random.fold_in(key, 11)
    shape = (LAYERS, TOKENS, D)
    value = mixture_drawn(key, shape, (LAYERS, 1, D))
    return jnp.clip(value, -8.0, 8.0).astype(jnp.bfloat16)


def draw_out_grad(key, part):
    key = jax.random.fold_in(key, 19)
    shape = (LAYERS, TOKENS, D)
    value = mixture_drawn(key, shape, (LAYERS, 1, D))
    return jnp.clip(value, -8.0, 8.0).astype(jnp.bfloat16)


def draw_gate_pre(key, part):
    key = jax.random.fold_in(key, 13)
    shape = (LAYERS, TOKENS, FF)
    value = mixture_drawn(key, shape, (LAYERS, 1, FF))
    return jnp.clip(value, -8.0, 8.0).astype(jnp.bfloat16)


def draw_up_pre(key, part):
    key = jax.random.fold_in(key, 17)
    shape = (LAYERS, TOKENS, FF)
    position = jnp.arange(FF, dtype=jnp.float32) / FF
    value = mixture_drawn(key, shape, (LAYERS, 1, FF)) * (0.5 + 1.1 * position)
    return jnp.clip(value, -8.0, 8.0).astype(jnp.bfloat16)


def with_ends(values, stream_key, low, largest):
    dims = values.shape
    spot = [jax.random.randint(jax.random.fold_in(stream_key, axis), (), 0, dims[axis]) for axis in range(len(dims))]
    values = values.at[tuple(spot)].set(low)
    longest = dims.index(max(dims))
    spot[longest] = (spot[longest] + 1) % dims[longest]
    return values.at[tuple(spot)].set(largest)


def block_scale(key, dims, pieces, smallest, top_value):
    gain = 1.0
    for dim, shards_of in pieces:
        steps = jax.random.uniform(jax.random.fold_in(jax.random.fold_in(key, 6), dim), (shards_of,), jnp.float32, smallest / len(pieces), top_value / len(pieces))
        gain = gain * jnp.repeat(jnp.exp(steps), dims[dim] // shards_of).reshape((-1,) + (1,) * (len(dims) - 1 - dim))
    return gain


def profile(count, total, most, lean):
    weights = [(1 << 20) // math.isqrt(standing ** lean) + 1 for standing in range(2, count + 1)]
    spare, given = total - most - (count - 1), [1] * (count - 1)
    while spare > 0:
        free = [i for i in range(count - 1) if given[i] < most]
        whole, left = sum([weights[i] for i in free]), spare
        for i in free:
            addition = min(most - given[i], max(1, left * weights[i] // whole), spare)
            given[i] = given[i] + addition
            spare = spare - addition
    return np.array([most] + given)


def uneven(stream_key, number_of, total, bound, slope):
    if number_of == 2:
        one = jax.random.randint(stream_key, (), max(1, total - bound), min(bound, total - 1) + 1)
        return jnp.stack([one, total - one])
    sizes = jnp.asarray(profile(number_of, total, bound, slope), jnp.int32)
    pairs = (number_of - 1) // 2
    giver, sink = sizes[1:1 + 2 * pairs:2], sizes[2:2 + 2 * pairs:2]
    slack = jnp.minimum(giver - 1, bound - sink)
    passed = jax.random.randint(jax.random.fold_in(stream_key, 1), (pairs,), 0, 1 << 20) % (slack + 1)
    sizes = sizes.at[1:1 + 2 * pairs:2].set(giver - passed).at[2:2 + 2 * pairs:2].set(sink + passed)
    return sizes[jax.random.permutation(jax.random.fold_in(stream_key, 2), number_of)]


def bell_draw(key, shape, width, bound, cuts=(), held_as=jnp.bfloat16):
    array = jax.random.normal(key, shape, jnp.float32) * width
    if len(cuts) > 0:
        array = block_scale(key, shape, cuts, -0.22, 0.18) * array
    return jnp.clip(array, min=-bound, max=bound).astype(held_as)


def setup_inputs(seed: int = 0) -> dict:
    splits = jax.random.split(jax.random.key(seed), 13)
    return {
        "inputs": draw_inputs(jax.random.fold_in(splits[12], 71), 0),
        "out_grad": draw_out_grad(jax.random.fold_in(splits[12], 71), 0),
        "gate_pre": draw_gate_pre(jax.random.fold_in(splits[12], 71), 0),
        "up_pre": draw_up_pre(jax.random.fold_in(splits[12], 71), 0),
        "gate_weight": bell_draw(splits[4], (LAYERS, D, FF), D ** -0.5, 0.125, ((0, 2), (1, 8), (2, 16))),
        "up_weight": bell_draw(splits[5], (LAYERS, D, FF), D ** -0.5, 0.125, ((0, 2), (1, 8), (2, 16))),
        "down_weight": bell_draw(splits[6], (LAYERS, D, FF), FF ** -0.5, 0.046875, ((0, 2), (1, 8), (2, 16))),
        "noise_gate": bell_draw(splits[7], (LAYERS, D, FF), (8 * EXAMPLES), 768.0, ((0, 2), (1, 8), (2, 16))),
        "noise_up": bell_draw(splits[8], (LAYERS, D, FF), (8 * EXAMPLES), 768.0, ((0, 2), (1, 8), (2, 16))),
        "noise_down": bell_draw(splits[9], (LAYERS, D, FF), (8 * EXAMPLES), 768.0, ((0, 2), (1, 8), (2, 16))),
        "example_of_block": jax.vmap(lambda own: jnp.searchsorted(jnp.cumsum(uneven(own, EX_DEV, NB, MOST_BLOCKS, 0)), jnp.arange(NB), side="right"))(jax.random.split(splits[10], DP_GROUPS)).reshape((DP_GROUPS, NB)).astype(jnp.int32),
        "tail_tokens": with_ends(jax.random.randint(splits[11], (EXAMPLES,), 1, BLOCK + 1), jax.random.fold_in(splits[11], 1), 1, BLOCK).astype(jnp.int32),
    }


def gram_matrix(matrix):
    return jnp.dot(matrix, matrix.T, preferred_element_type=jnp.float32)

def example_sums(products, member):
    blocks = member.shape[0]
    span_rows = products.shape[0] // blocks
    summed = products.reshape(blocks, span_rows, blocks, span_rows).sum(axis=(1, 3))
    return lax.optimization_barrier(jnp.sum(member * lax.optimization_barrier(jnp.sum(summed[:, :, None] * member[None, :, :], axis=1)), axis=0))

def reference(inputs, out_grad, gate_pre, up_pre, gate_weight, up_weight, down_weight, noise_gate, noise_up, noise_down, example_of_block, tail_tokens):
    tails = tail_tokens.reshape(N_DP, EX_DEV)
    member = example_of_block[:, :, None] == jnp.arange(EX_DEV, dtype=jnp.int32)[None, None, :]
    following = jnp.concatenate([example_of_block[:, 1:], jnp.full((N_DP, 1), -1, jnp.int32)], axis=1)
    closing = following != example_of_block
    block_tail = lax.optimization_barrier(jnp.sum(jnp.where(member, tails[:, None, :], 0), axis=2))
    offsets = jnp.arange(BLOCK, dtype=jnp.int32)
    present = jnp.where(closing[:, :, None], offsets[None, None, :] < block_tail[:, :, None], True).reshape(TOKENS)
    membership = member.astype(jnp.float32)
    owner = example_of_block + jnp.arange(N_DP, dtype=jnp.int32)[:, None] * EX_DEV
    token_owner = jnp.repeat(owner.reshape(-1), BLOCK)
    hidden_share = FF // N_TENSOR
    squares = jnp.zeros((N_DP, EX_DEV), jnp.float32)
    input_grads = []
    saved = []
    for layer in range(LAYERS):
        layer_in = inputs[layer]
        masked = out_grad[layer] * present.astype(jnp.bfloat16)[:, None]
        back = jnp.dot(masked, down_weight[layer], preferred_element_type=jnp.float32)
        gate_f = gate_pre[layer].astype(jnp.float32)
        up_f = up_pre[layer].astype(jnp.float32)
        sigmoid_gate = jax.nn.sigmoid(gate_f)
        activated = gate_f * sigmoid_gate
        hidden = (activated * up_f).astype(jnp.bfloat16)
        up_cot = (back * activated).astype(jnp.bfloat16)
        gate_cot = (back * up_f * sigmoid_gate * (1.0 + gate_f * (1.0 - sigmoid_gate))).astype(jnp.bfloat16)
        gate_w = gate_weight[layer]
        up_w = up_weight[layer]

        def add_part(running, group):
            anchor = group * hidden_share
            gate_block = lax.dynamic_slice_in_dim(gate_cot, anchor, hidden_share, 1)
            up_block = lax.dynamic_slice_in_dim(up_cot, anchor, hidden_share, 1)
            gate_rows = lax.dynamic_slice_in_dim(gate_w, anchor, hidden_share, 1)
            up_rows = lax.dynamic_slice_in_dim(up_w, anchor, hidden_share, 1)
            product = jnp.dot(gate_block, gate_rows.T, preferred_element_type=jnp.float32) + jnp.dot(up_block, up_rows.T, preferred_element_type=jnp.float32)
            return (running + lax.optimization_barrier(product.astype(jnp.bfloat16)).astype(jnp.float32), None)
        summed_in, _ = lax.scan(add_part, jnp.zeros((TOKENS, D), jnp.float32), jnp.arange(N_TENSOR, dtype=jnp.int32))
        input_grads.append(summed_in.astype(jnp.bfloat16))
        cotangents = jnp.concatenate([gate_cot, up_cot], axis=1)

        def group_norm(group):
            anchor = group * TOK_DEV
            in_rows = lax.dynamic_slice_in_dim(layer_in, anchor, TOK_DEV, 0)
            cot_rows = lax.dynamic_slice_in_dim(cotangents, anchor, TOK_DEV, 0)
            hid_rows = lax.dynamic_slice_in_dim(hidden, anchor, TOK_DEV, 0)
            out_rows = lax.dynamic_slice_in_dim(masked, anchor, TOK_DEV, 0)
            products = gram_matrix(in_rows) * gram_matrix(cot_rows) + gram_matrix(hid_rows) * gram_matrix(out_rows)
            return example_sums(products, lax.dynamic_index_in_dim(membership, group, 0, keepdims=False))
        squares = squares + lax.map(group_norm, jnp.arange(N_DP, dtype=jnp.int32))
        saved.append((layer_in, masked, hidden, gate_cot, up_cot))
    clip_bound = 32.0 * math.sqrt(D * FF)
    norm_ratio = (jnp.sqrt(squares) / clip_bound).reshape(EXAMPLES)
    factor = 1.0 / jnp.maximum(norm_ratio, 1.0)
    token_factor = factor[token_owner][:, None]
    scaling = 1.0 / (32.0 * EXAMPLES)
    grads_gate = []
    grads_up = []
    grads_down = []
    for layer in range(LAYERS):
        layer_in, masked, hidden, gate_cot, up_cot = saved[layer]
        scaled_gate = (token_factor * gate_cot.astype(jnp.float32)).astype(jnp.bfloat16)
        scaled_up = (token_factor * up_cot.astype(jnp.float32)).astype(jnp.bfloat16)
        scaled_out = (token_factor * masked.astype(jnp.float32)).astype(jnp.bfloat16)

        def add_group(running, group):
            anchor = group * TOK_DEV
            in_rows = lax.dynamic_slice_in_dim(layer_in, anchor, TOK_DEV, 0)
            out_rows = lax.dynamic_slice_in_dim(scaled_out, anchor, TOK_DEV, 0)
            gate_rows = lax.dynamic_slice_in_dim(scaled_gate, anchor, TOK_DEV, 0)
            up_rows = lax.dynamic_slice_in_dim(scaled_up, anchor, TOK_DEV, 0)
            hid_rows = lax.dynamic_slice_in_dim(hidden, anchor, TOK_DEV, 0)
            terms = (jnp.dot(in_rows.T, gate_rows, preferred_element_type=jnp.float32), jnp.dot(in_rows.T, up_rows, preferred_element_type=jnp.float32), jnp.dot(out_rows.T, hid_rows, preferred_element_type=jnp.float32))
            return (tuple((value + lax.optimization_barrier(term.astype(jnp.bfloat16)).astype(jnp.float32) for value, term in zip(running, terms))), None)
        zeros = jnp.zeros((D, FF), jnp.float32)
        sums, _ = lax.scan(add_group, (zeros, zeros, zeros), jnp.arange(N_DP, dtype=jnp.int32))
        grads_gate.append(((sums[0] + noise_gate[layer].astype(jnp.float32)) * scaling).astype(jnp.bfloat16))
        grads_up.append(((sums[1] + noise_up[layer].astype(jnp.float32)) * scaling).astype(jnp.bfloat16))
        grads_down.append(((sums[2] + noise_down[layer].astype(jnp.float32)) * scaling).astype(jnp.bfloat16))
    return (jnp.stack(input_grads), jnp.stack(grads_gate), jnp.stack(grads_up), jnp.stack(grads_down), norm_ratio)
```

```python
import math

import jax
import jax.numpy as jnp
from jax import lax
from jax.sharding import PartitionSpec as P

D = 2304
FF = 18432
BLOCK = 128
CORES = 2
PLANES = 4
SIDE = 4


def from_plane(value, distance):
    pairs = [
        (((plane + distance) % PLANES) * CORES + core, plane * CORES + core)
        for plane in range(PLANES)
        for core in range(CORES)
    ]
    return lax.ppermute(value, "dp", pairs)


def from_other_core(value):
    return lax.ppermute(value, "dp", [(d, d ^ 1) for d in range(PLANES * CORES)])


def along_x(value, distance):
    pairs = [
        (x * SIDE + y, ((x + distance) % SIDE) * SIDE + y) for x in range(SIDE) for y in range(SIDE)
    ]
    return lax.ppermute(value, "tensor", pairs)


def along_y(value, distance):
    pairs = [
        (x * SIDE + y, x * SIDE + (y + distance) % SIDE) for x in range(SIDE) for y in range(SIDE)
    ]
    return lax.ppermute(value, "tensor", pairs)


def paired_sum(value):
    for mask in (1, 2, 4, 8):
        value = value + lax.ppermute(value, "tensor", [(t, t ^ mask) for t in range(SIDE * SIDE)])
    return value + lax.ppermute(value, "pipe", [(0, 1), (1, 0)])


def block_layout(example_row, tail_local):
    quantity = tail_local.shape[0]
    member = example_row[:, None] == jnp.arange(quantity, dtype=jnp.int32)[None, :]
    following = jnp.concatenate([example_row[1:], jnp.full((1,), -1, jnp.int32)])
    closing = following != example_row
    block_tail = jnp.sum(jnp.where(member, tail_local[None, :], 0), axis=1)
    offsets = jnp.arange(BLOCK, dtype=jnp.int32)
    present = jnp.where(closing[:, None], offsets[None, :] < block_tail[:, None], True)
    return (member.astype(jnp.float32), present.reshape(-1))


def gram_matrix(matrix):
    return jnp.einsum("td,sd->ts", matrix, matrix, preferred_element_type=jnp.float32)


def example_sums(products, member):
    blocks = member.shape[0]
    span_rows = products.shape[0] // blocks
    summed = products.reshape(blocks, span_rows, blocks, span_rows).sum(axis=(1, 3))
    return jnp.sum(member * jnp.sum(summed[:, :, None] * member[None, :, :], axis=1), axis=0)


def contract(left, right):
    return jnp.einsum("tk,tj->kj", left, right, preferred_element_type=jnp.float32)


def gather_ring(own):
    half = own.shape[0] // 2
    after = from_plane(own, 1)
    before = from_plane(own, 3)
    far_low = from_plane(after[:half], 1)
    far_high = from_plane(before[half:], 3)
    return own, after, (far_low, far_high), before


def cotangents(masked, down, gate, up):
    back = jnp.dot(masked, down, preferred_element_type=jnp.float32)
    gate_f = gate.astype(jnp.float32)
    up_f = up.astype(jnp.float32)
    sigmoid_gate = jax.nn.sigmoid(gate_f)
    activated = gate_f * sigmoid_gate
    hidden = (activated * up_f).astype(jnp.bfloat16)
    up_cot = (back * activated).astype(jnp.bfloat16)
    gate_cot = (back * up_f * sigmoid_gate * (1.0 + gate_f * (1.0 - sigmoid_gate))).astype(
        jnp.bfloat16
    )
    return gate_cot, up_cot, hidden


def scatter_sum(value):
    groups, _, rows, columns = value.shape
    index = lax.axis_index("tensor")
    x, y = index // SIDE, index % SIDE
    value = value.reshape(groups, SIDE, SIDE, rows, columns)

    def stage(value, place, move, axis):
        def block(at):
            return lax.dynamic_index_in_dim(value, at % SIDE, axis, keepdims=False)

        total = block(place).astype(jnp.float32)
        for distance in (1, 2, 3):
            total = total + move(block(place + distance), distance).astype(jnp.float32)
        return total.astype(jnp.bfloat16)

    return stage(stage(value, x, along_x, 1), y, along_y, 1)


def shards(
    inputs,
    out_grad,
    gate_pre,
    up_pre,
    gate_weight,
    up_weight,
    down_weight,
    noise_gate,
    noise_up,
    noise_down,
    example_of_block,
    tail_tokens,
):
    layer_in = inputs[0]
    tokens = layer_in.shape[0]
    rows = down_weight.shape[1]
    span = CORES * rows
    dp = lax.axis_index("dp")
    plane, core = dp // CORES, dp % CORES
    place = lax.axis_index("tensor")
    slice_rows = tokens // (SIDE * SIDE)

    member, present = block_layout(example_of_block[0], tail_tokens)
    masked = out_grad[0] * present.astype(jnp.bfloat16)[:, None]

    def own_span(matrix, at):
        return lax.dynamic_slice_in_dim(matrix, (at % PLANES) * span, span, 1)

    masked_piece = lax.dynamic_slice_in_dim(masked, place * slice_rows, slice_rows, 0)
    inputs_piece = lax.dynamic_slice_in_dim(layer_in, place * slice_rows, slice_rows, 0)
    masked_of, inputs_of, scaled_side = [masked], [own_span(layer_in, plane)], [own_span(masked, plane)]
    received = lax.optimization_barrier(
        [
            from_plane(
                jnp.concatenate([masked_piece, own_span(inputs_piece, plane - distance)], axis=1),
                distance,
            )
            for distance in (1, 2, 3)
        ]
    )
    for got in received:
        got = jnp.concatenate([got, own_span(got[:, :D], plane)], axis=1)
        whole = lax.all_gather(got, "tensor", axis=0, tiled=True)
        masked_of.append(whole[:, :D])
        inputs_of.append(whole[:, D : D + span])
        scaled_side.append(whole[:, D + span :])

    down_ring = gather_ring(down_weight[0])
    down_here = [down_ring[0], down_ring[1], jnp.concatenate(down_ring[2], axis=0), down_ring[3]]
    down = jnp.zeros((PLANES * CORES,) + down_weight.shape[1:], jnp.bfloat16)
    for distance, piece in enumerate(down_here):
        at = ((plane + distance) % PLANES) * CORES
        down = lax.dynamic_update_index_in_dim(down, piece, at + core, 0)
        down = lax.dynamic_update_index_in_dim(down, from_other_core(piece), at + 1 - core, 0)
    down = down.reshape(D, down_weight.shape[2])

    def both_cores(own):
        other = from_other_core(own)
        first = core == 0
        return jnp.concatenate([jnp.where(first, own, other), jnp.where(first, other, own)], axis=0)

    gate_rows = both_cores(gate_weight[0])
    up_rows = both_cores(up_weight[0])

    gate_own, _ = lax.optimization_barrier((gate_pre[0], (down_ring[1], down_ring[3])))
    gate_ring = gather_ring(gate_own)
    up_own, _ = lax.optimization_barrier((up_pre[0], down_ring[2]))
    up_ring = gather_ring(up_own)

    gate_cot, up_cot, hidden = cotangents(masked, down, gate_pre[0], up_pre[0])
    cots = jnp.concatenate([gate_cot, up_cot], axis=1)
    products = gram_matrix(layer_in) * gram_matrix(cots) + gram_matrix(hidden) * gram_matrix(masked)
    squares = paired_sum(example_sums(products, member))
    norm_ratio = jnp.sqrt(squares) / (32.0 * math.sqrt(D * FF))
    factor = 1.0 / jnp.maximum(norm_ratio, 1.0)
    block_factor = jnp.sum(member * factor[None, :], axis=1)

    def scaled(matrix, factors):
        return (jnp.repeat(factors, BLOCK)[:, None] * matrix.astype(jnp.float32)).astype(jnp.bfloat16)

    grads = [0.0, 0.0, 0.0]
    shares = {}
    for distance in (0, 1, 3, 2):
        if distance:
            gate, up = gate_ring[distance], up_ring[distance]
            if distance == 2:
                (gate, up), grads, shares = lax.optimization_barrier(((gate, up), grads, shares))
                near = scatter_sum(jnp.stack([shares[0], shares[1], shares[3]]))
                gate, up = jnp.concatenate(gate, axis=0), jnp.concatenate(up, axis=0)
            gate_cot, up_cot, hidden = cotangents(masked_of[distance], down, gate, up)
        share = jnp.einsum("tj,kj->tk", gate_cot, gate_rows, preferred_element_type=jnp.float32)
        share = share + jnp.einsum("tj,kj->tk", up_cot, up_rows, preferred_element_type=jnp.float32)
        shares[distance] = share.astype(jnp.bfloat16).reshape(SIDE * SIDE, slice_rows, span)
        factors = from_plane(block_factor, distance) if distance else block_factor
        in_scaled = scaled(inputs_of[distance], factors)
        out_scaled = scaled(scaled_side[distance], factors)
        grads[0] = grads[0] + contract(in_scaled, gate_cot)
        grads[1] = grads[1] + contract(in_scaled, up_cot)
        grads[2] = grads[2] + contract(out_scaled, hidden)

    far = scatter_sum(shares[2][None])
    summed = [near[0], from_plane(near[2], 1), from_plane(far[0], 2), from_plane(near[1], 3)]
    input_grad = jnp.zeros((slice_rows, PLANES, span), jnp.bfloat16)
    for distance, piece in enumerate(summed):
        input_grad = lax.dynamic_update_index_in_dim(input_grad, piece, (plane + distance) % PLANES, 1)
    input_grad = input_grad.reshape(1, slice_rows, D)

    scaling = 1.0 / (32.0 * tail_tokens.shape[0] * lax.axis_size("dp"))
    results = []
    for grad, noise in zip(grads, (noise_gate, noise_up, noise_down)):
        kept = lax.dynamic_slice_in_dim(grad, core * rows, rows, 0)
        given = lax.dynamic_slice_in_dim(grad, (1 - core) * rows, rows, 0).astype(jnp.bfloat16)
        total = kept + from_other_core(given).astype(jnp.float32)
        results.append(((total + noise[0].astype(jnp.float32)) * scaling).astype(jnp.bfloat16)[None])
    return (input_grad, *results, norm_ratio)


def solution(mesh):
    weight = P("pipe", "dp", "tensor")
    in_specs = (P("pipe", "dp", None),) * 2 + (weight,) * 8 + (P("dp", None), P("dp"))
    out_specs = (P("pipe", ("dp", "tensor"), None), weight, weight, weight, P("dp"))
    return jax.shard_map(shards, mesh=mesh, in_specs=in_specs, out_specs=out_specs, check_vma=False)
```

```python
import math

import jax
import jax.numpy as jnp
from jax import lax
from jax.sharding import PartitionSpec as P

D = 2304
FF = 18432
BLOCK = 128
CORES = 2
PLANES = 4
SIDE = 4


def from_plane(value, distance):
    pairs = [
        (((plane + distance) % PLANES) * CORES + core, plane * CORES + core)
        for plane in range(PLANES)
        for core in range(CORES)
    ]
    return lax.ppermute(value, "dp", pairs)


def from_other_core(value):
    return lax.ppermute(value, "dp", [(d, d ^ 1) for d in range(PLANES * CORES)])


def along_x(value, distance):
    pairs = [
        (x * SIDE + y, ((x + distance) % SIDE) * SIDE + y) for x in range(SIDE) for y in range(SIDE)
    ]
    return lax.ppermute(value, "tensor", pairs)


def along_y(value, distance):
    pairs = [
        (x * SIDE + y, x * SIDE + (y + distance) % SIDE) for x in range(SIDE) for y in range(SIDE)
    ]
    return lax.ppermute(value, "tensor", pairs)


def paired_sum(value):
    for mask in (1, 2, 4, 8):
        value = value + lax.ppermute(value, "tensor", [(t, t ^ mask) for t in range(SIDE * SIDE)])
    return value + lax.ppermute(value, "pipe", [(0, 1), (1, 0)])


def block_layout(example_row, tail_local):
    quantity = tail_local.shape[0]
    member = example_row[:, None] == jnp.arange(quantity, dtype=jnp.int32)[None, :]
    following = jnp.concatenate([example_row[1:], jnp.full((1,), -1, jnp.int32)])
    closing = following != example_row
    block_tail = jnp.sum(jnp.where(member, tail_local[None, :], 0), axis=1)
    offsets = jnp.arange(BLOCK, dtype=jnp.int32)
    present = jnp.where(closing[:, None], offsets[None, :] < block_tail[:, None], True)
    return (member.astype(jnp.float32), present.reshape(-1))


def gram_matrix(matrix):
    return jnp.einsum("td,sd->ts", matrix, matrix, preferred_element_type=jnp.float32)


def example_sums(products, member):
    blocks = member.shape[0]
    span_rows = products.shape[0] // blocks
    summed = products.reshape(blocks, span_rows, blocks, span_rows).sum(axis=(1, 3))
    return jnp.sum(member * jnp.sum(summed[:, :, None] * member[None, :, :], axis=1), axis=0)


def contract(left, right):
    return jnp.einsum("tk,tj->kj", left, right, preferred_element_type=jnp.float32)


def to_neighbours(own):
    return from_plane(own, 1), from_plane(own, 3)


def to_far(after, before):
    half = after.shape[0] // 2
    return from_plane(after[:half], 1), from_plane(before[half:], 3)


def cotangents(masked, down, gate, up):
    back = jnp.dot(masked, down, preferred_element_type=jnp.float32)
    gate_f = gate.astype(jnp.float32)
    up_f = up.astype(jnp.float32)
    sigmoid_gate = jax.nn.sigmoid(gate_f)
    activated = gate_f * sigmoid_gate
    hidden = (activated * up_f).astype(jnp.bfloat16)
    up_cot = (back * activated).astype(jnp.bfloat16)
    gate_cot = (back * up_f * sigmoid_gate * (1.0 + gate_f * (1.0 - sigmoid_gate))).astype(
        jnp.bfloat16
    )
    return gate_cot, up_cot, hidden


def scatter_sum(value):
    groups, _, rows, columns = value.shape
    index = lax.axis_index("tensor")
    x, y = index // SIDE, index % SIDE
    value = value.reshape(groups, SIDE, SIDE, rows, columns)

    def stage(value, place, move, axis):
        def block(at):
            return lax.dynamic_index_in_dim(value, at % SIDE, axis, keepdims=False)

        total = block(place).astype(jnp.float32)
        for distance in (1, 2, 3):
            total = total + move(block(place + distance), distance).astype(jnp.float32)
        return total.astype(jnp.bfloat16)

    return stage(stage(value, x, along_x, 1), y, along_y, 1)


def shards(
    inputs,
    out_grad,
    gate_pre,
    up_pre,
    gate_weight,
    up_weight,
    down_weight,
    noise_gate,
    noise_up,
    noise_down,
    example_of_block,
    tail_tokens,
):
    layer_in = inputs[0]
    tokens = layer_in.shape[0]
    rows = down_weight.shape[1]
    span = CORES * rows
    dp = lax.axis_index("dp")
    plane, core = dp // CORES, dp % CORES
    place = lax.axis_index("tensor")
    slice_rows = tokens // (SIDE * SIDE)

    member, present = block_layout(example_of_block[0], tail_tokens)
    masked = out_grad[0] * present.astype(jnp.bfloat16)[:, None]

    def own_span(matrix, at):
        return lax.dynamic_slice_in_dim(matrix, (at % PLANES) * span, span, 1)

    masked_piece = lax.dynamic_slice_in_dim(masked, place * slice_rows, slice_rows, 0)
    inputs_piece = lax.dynamic_slice_in_dim(layer_in, place * slice_rows, slice_rows, 0)
    received = [
        from_plane(
            jnp.concatenate([masked_piece, own_span(inputs_piece, plane - distance)], axis=1),
            distance,
        )
        for distance in (1, 2, 3)
    ]
    down_near = to_neighbours(down_weight[0])
    received, down_near = lax.optimization_barrier((received, down_near))
    down_far = to_far(*down_near)
    masked_of, inputs_of, scaled_side = [masked], [own_span(layer_in, plane)], [own_span(masked, plane)]
    for got in received:
        got = jnp.concatenate([got, own_span(got[:, :D], plane)], axis=1)
        whole = lax.all_gather(got, "tensor", axis=0, tiled=True)
        masked_of.append(whole[:, :D])
        inputs_of.append(whole[:, D : D + span])
        scaled_side.append(whole[:, D + span :])

    width = gate_pre.shape[2]
    pre_own = jnp.concatenate([gate_pre[0], up_pre[0]], axis=1)
    pre_own, down_far = lax.optimization_barrier((pre_own, down_far))
    pre_near = to_neighbours(pre_own)
    down_here = [down_weight[0], down_near[0], jnp.concatenate(down_far, axis=0), down_near[1]]
    down = jnp.zeros((PLANES * CORES,) + down_weight.shape[1:], jnp.bfloat16)
    for distance, piece in enumerate(down_here):
        at = ((plane + distance) % PLANES) * CORES
        down = lax.dynamic_update_index_in_dim(down, piece, at + core, 0)
        down = lax.dynamic_update_index_in_dim(down, from_other_core(piece), at + 1 - core, 0)
    down = down.reshape(D, down_weight.shape[2])

    def both_cores(own):
        other = from_other_core(own)
        first = core == 0
        return jnp.concatenate([jnp.where(first, own, other), jnp.where(first, other, own)], axis=0)

    gate_rows = both_cores(gate_weight[0])
    up_rows = both_cores(up_weight[0])

    gate_cot, up_cot, hidden = cotangents(masked, down, gate_pre[0], up_pre[0])
    cots = jnp.concatenate([gate_cot, up_cot], axis=1)
    products = gram_matrix(layer_in) * gram_matrix(cots) + gram_matrix(hidden) * gram_matrix(masked)
    squares = paired_sum(example_sums(products, member))
    norm_ratio = jnp.sqrt(squares) / (32.0 * math.sqrt(D * FF))
    factor = 1.0 / jnp.maximum(norm_ratio, 1.0)
    block_factor = jnp.sum(member * factor[None, :], axis=1)

    def scaled(matrix, factors):
        return (jnp.repeat(factors, BLOCK)[:, None] * matrix.astype(jnp.float32)).astype(jnp.bfloat16)

    def share_of(gate_cot, up_cot):
        share = jnp.einsum("tj,kj->tk", gate_cot, gate_rows, preferred_element_type=jnp.float32)
        share = share + jnp.einsum("tj,kj->tk", up_cot, up_rows, preferred_element_type=jnp.float32)
        return share.astype(jnp.bfloat16).reshape(SIDE * SIDE, slice_rows, span)

    def grads_of(distance, cots):
        gate_cot, up_cot, hidden = cots
        in_scaled = scaled(inputs_of[distance], factors[distance])
        out_scaled = scaled(scaled_side[distance], factors[distance])
        return [
            contract(in_scaled, gate_cot),
            contract(in_scaled, up_cot),
            contract(out_scaled, hidden),
        ]

    def summed(*grads):
        return [sum(parts[1:], parts[0]) for parts in zip(*grads)]

    factors = [block_factor] + [from_plane(block_factor, distance) for distance in (1, 2, 3)]
    grads = grads_of(0, (gate_cot, up_cot, hidden))
    kept = scatter_sum(share_of(gate_cot, up_cot)[None])
    pre_near, factors, grads, kept = lax.optimization_barrier((pre_near, factors, grads, kept))
    pre_far = to_far(*pre_near)
    after = cotangents(masked_of[1], down, pre_near[0][:, :width], pre_near[0][:, width:])
    before = cotangents(masked_of[3], down, pre_near[1][:, :width], pre_near[1][:, width:])
    shares = jnp.stack([share_of(*after[:2]), share_of(*before[:2])])
    grads = summed(grads, grads_of(1, after), grads_of(3, before))
    near = scatter_sum(shares)
    pre_far, grads, near = lax.optimization_barrier((pre_far, grads, near))
    pre_far = jnp.concatenate(pre_far, axis=0)
    beyond = cotangents(masked_of[2], down, pre_far[:, :width], pre_far[:, width:])
    grads = summed(grads, grads_of(2, beyond))
    far = scatter_sum(share_of(*beyond[:2])[None])
    pieces = [kept[0], from_plane(near[1], 1), from_plane(far[0], 2), from_plane(near[0], 3)]
    input_grad = jnp.zeros((slice_rows, PLANES, span), jnp.bfloat16)
    for distance, piece in enumerate(pieces):
        input_grad = lax.dynamic_update_index_in_dim(input_grad, piece, (plane + distance) % PLANES, 1)
    input_grad = input_grad.reshape(1, slice_rows, D)

    scaling = 1.0 / (32.0 * tail_tokens.shape[0] * lax.axis_size("dp"))
    results = []
    for grad, noise in zip(grads, (noise_gate, noise_up, noise_down)):
        held = lax.dynamic_slice_in_dim(grad, core * rows, rows, 0)
        given = lax.dynamic_slice_in_dim(grad, (1 - core) * rows, rows, 0).astype(jnp.bfloat16)
        total = held + from_other_core(given).astype(jnp.float32)
        results.append(((total + noise[0].astype(jnp.float32)) * scaling).astype(jnp.bfloat16)[None])
    return (input_grad, *results, norm_ratio)


def solution(mesh):
    weight = P("pipe", "dp", "tensor")
    in_specs = (P("pipe", "dp", None),) * 2 + (weight,) * 8 + (P("dp", None), P("dp"))
    out_specs = (P("pipe", ("dp", "tensor"), None), weight, weight, weight, P("dp"))
    return jax.shard_map(shards, mesh=mesh, in_specs=in_specs, out_specs=out_specs, check_vma=False)
```

```python
import math

import jax
import jax.numpy as jnp
from jax import lax
from jax.sharding import PartitionSpec as P

D = 2304
FF = 18432
BLOCK = 128
CORES = 2
PLANES = 4
SIDE = 4


def from_plane(value, distance):
    pairs = [
        (((plane + distance) % PLANES) * CORES + core, plane * CORES + core)
        for plane in range(PLANES)
        for core in range(CORES)
    ]
    return lax.ppermute(value, "dp", pairs)


def from_other_core(value):
    return lax.ppermute(value, "dp", [(d, d ^ 1) for d in range(PLANES * CORES)])


def along_x(value, distance):
    pairs = [
        (x * SIDE + y, ((x + distance) % SIDE) * SIDE + y) for x in range(SIDE) for y in range(SIDE)
    ]
    return lax.ppermute(value, "tensor", pairs)


def along_y(value, distance):
    pairs = [
        (x * SIDE + y, x * SIDE + (y + distance) % SIDE) for x in range(SIDE) for y in range(SIDE)
    ]
    return lax.ppermute(value, "tensor", pairs)


def paired_sum(value):
    for mask in (1, 2, 4, 8):
        value = value + lax.ppermute(value, "tensor", [(t, t ^ mask) for t in range(SIDE * SIDE)])
    return value + lax.ppermute(value, "pipe", [(0, 1), (1, 0)])


def block_layout(example_row, tail_local):
    quantity = tail_local.shape[0]
    member = example_row[:, None] == jnp.arange(quantity, dtype=jnp.int32)[None, :]
    following = jnp.concatenate([example_row[1:], jnp.full((1,), -1, jnp.int32)])
    closing = following != example_row
    block_tail = jnp.sum(jnp.where(member, tail_local[None, :], 0), axis=1)
    offsets = jnp.arange(BLOCK, dtype=jnp.int32)
    present = jnp.where(closing[:, None], offsets[None, :] < block_tail[:, None], True)
    return (member.astype(jnp.float32), present.reshape(-1))


def gram_matrix(matrix):
    return jnp.einsum("td,sd->ts", matrix, matrix, preferred_element_type=jnp.float32)


def example_sums(products, member):
    blocks = member.shape[0]
    span_rows = products.shape[0] // blocks
    summed = products.reshape(blocks, span_rows, blocks, span_rows).sum(axis=(1, 3))
    return jnp.sum(member * jnp.sum(summed[:, :, None] * member[None, :, :], axis=1), axis=0)


def contract(left, right):
    return jnp.einsum("tk,tj->kj", left, right, preferred_element_type=jnp.float32)


def to_neighbours(own):
    return from_plane(own, 1), from_plane(own, 3)


def to_far(after, before):
    half = after.shape[0] // 2
    return from_plane(after[:half], 1), from_plane(before[half:], 3)


def cotangents(masked, down, gate, up):
    back = jnp.dot(masked, down, preferred_element_type=jnp.float32)
    gate_f = gate.astype(jnp.float32)
    up_f = up.astype(jnp.float32)
    sigmoid_gate = jax.nn.sigmoid(gate_f)
    activated = gate_f * sigmoid_gate
    hidden = (activated * up_f).astype(jnp.bfloat16)
    up_cot = (back * activated).astype(jnp.bfloat16)
    gate_cot = (back * up_f * sigmoid_gate * (1.0 + gate_f * (1.0 - sigmoid_gate))).astype(
        jnp.bfloat16
    )
    return gate_cot, up_cot, hidden


def scatter_sum(value):
    groups, _, rows, columns = value.shape
    index = lax.axis_index("tensor")
    x, y = index // SIDE, index % SIDE
    value = value.reshape(groups, SIDE, SIDE, rows, columns)

    def stage(value, place, move, axis):
        def block(at):
            return lax.dynamic_index_in_dim(value, at % SIDE, axis, keepdims=False)

        total = block(place).astype(jnp.float32)
        for distance in (1, 2, 3):
            total = total + move(block(place + distance), distance).astype(jnp.float32)
        return total.astype(jnp.bfloat16)

    return stage(stage(value, x, along_x, 1), y, along_y, 1)


def shards(
    inputs,
    out_grad,
    gate_pre,
    up_pre,
    gate_weight,
    up_weight,
    down_weight,
    noise_gate,
    noise_up,
    noise_down,
    example_of_block,
    tail_tokens,
):
    layer_in = inputs[0]
    tokens = layer_in.shape[0]
    rows = down_weight.shape[1]
    span = CORES * rows
    dp = lax.axis_index("dp")
    plane, core = dp // CORES, dp % CORES
    place = lax.axis_index("tensor")
    slice_rows = tokens // (SIDE * SIDE)

    member, present = block_layout(example_of_block[0], tail_tokens)
    masked = out_grad[0] * present.astype(jnp.bfloat16)[:, None]

    def own_span(matrix, at):
        return lax.dynamic_slice_in_dim(matrix, (at % PLANES) * span, span, 1)

    masked_piece = lax.dynamic_slice_in_dim(masked, place * slice_rows, slice_rows, 0)
    inputs_piece = lax.dynamic_slice_in_dim(layer_in, place * slice_rows, slice_rows, 0)
    received = [
        from_plane(
            jnp.concatenate([masked_piece, own_span(inputs_piece, plane - distance)], axis=1),
            distance,
        )
        for distance in (1, 2, 3)
    ]
    down_near = to_neighbours(down_weight[0])
    width = gate_pre.shape[2]
    pre_own = jnp.concatenate([gate_pre[0], up_pre[0]], axis=1)
    empty = jnp.zeros((PLANES * CORES,) + down_weight.shape[1:], jnp.bfloat16)
    across = [from_other_core(own[0]) for own in (down_weight, gate_weight, up_weight)]
    received, down_near, across, pre_own, empty, gram_in, gram_out = lax.optimization_barrier(
        (received, down_near, across, pre_own, empty, gram_matrix(layer_in), gram_matrix(masked))
    )
    down_far = to_far(*down_near)
    masked_of, inputs_of, scaled_side = [masked], [own_span(layer_in, plane)], [own_span(masked, plane)]
    for got in received:
        got = jnp.concatenate([got, own_span(got[:, :D], plane)], axis=1)
        whole = lax.all_gather(got, "tensor", axis=0, tiled=True)
        masked_of.append(whole[:, :D])
        inputs_of.append(whole[:, D : D + span])
        scaled_side.append(whole[:, D + span :])

    pre_own, down_far = lax.optimization_barrier((pre_own, down_far))
    pre_near = to_neighbours(pre_own)
    down_here = [down_weight[0], down_near[0], jnp.concatenate(down_far, axis=0), down_near[1]]
    down = empty
    for distance, piece in enumerate(down_here):
        at = ((plane + distance) % PLANES) * CORES
        down = lax.dynamic_update_index_in_dim(down, piece, at + core, 0)
        other = from_other_core(piece) if distance else across[0]
        down = lax.dynamic_update_index_in_dim(down, other, at + 1 - core, 0)
    down = down.reshape(D, down_weight.shape[2])

    def both_cores(own, other):
        first = core == 0
        return jnp.concatenate([jnp.where(first, own, other), jnp.where(first, other, own)], axis=0)

    gate_rows = both_cores(gate_weight[0], across[1])
    up_rows = both_cores(up_weight[0], across[2])

    gate_cot, up_cot, hidden = cotangents(masked, down, gate_pre[0], up_pre[0])
    cots = jnp.concatenate([gate_cot, up_cot], axis=1)
    products = gram_in * gram_matrix(cots) + gram_matrix(hidden) * gram_out
    squares = paired_sum(example_sums(products, member))
    norm_ratio = jnp.sqrt(squares) / (32.0 * math.sqrt(D * FF))
    factor = 1.0 / jnp.maximum(norm_ratio, 1.0)
    block_factor = jnp.sum(member * factor[None, :], axis=1)

    def scaled(matrix, factors):
        return (jnp.repeat(factors, BLOCK)[:, None] * matrix.astype(jnp.float32)).astype(jnp.bfloat16)

    def share_of(gate_cot, up_cot):
        share = jnp.einsum("tj,kj->tk", gate_cot, gate_rows, preferred_element_type=jnp.float32)
        share = share + jnp.einsum("tj,kj->tk", up_cot, up_rows, preferred_element_type=jnp.float32)
        return share.astype(jnp.bfloat16).reshape(SIDE * SIDE, slice_rows, span)

    def grads_of(distance, cots):
        gate_cot, up_cot, hidden = cots
        in_scaled = scaled(inputs_of[distance], factors[distance])
        out_scaled = scaled(scaled_side[distance], factors[distance])
        return [
            contract(in_scaled, gate_cot),
            contract(in_scaled, up_cot),
            contract(out_scaled, hidden),
        ]

    def summed(*grads):
        return [sum(parts[1:], parts[0]) for parts in zip(*grads)]

    factors = [block_factor] + [from_plane(block_factor, distance) for distance in (1, 2, 3)]
    grads = grads_of(0, (gate_cot, up_cot, hidden))
    kept = scatter_sum(share_of(gate_cot, up_cot)[None])
    pre_near, grads, kept = lax.optimization_barrier((pre_near, grads, kept))
    pre_far = to_far(*pre_near)
    after = cotangents(masked_of[1], down, pre_near[0][:, :width], pre_near[0][:, width:])
    before = cotangents(masked_of[3], down, pre_near[1][:, :width], pre_near[1][:, width:])
    shares = jnp.stack([share_of(*after[:2]), share_of(*before[:2])])
    grads = summed(grads, grads_of(1, after), grads_of(3, before))
    near = scatter_sum(shares)
    pre_far, grads, near = lax.optimization_barrier((pre_far, grads, near))
    pre_far = jnp.concatenate(pre_far, axis=0)
    beyond = cotangents(masked_of[2], down, pre_far[:, :width], pre_far[:, width:])
    grads = summed(grads, grads_of(2, beyond))
    far = scatter_sum(share_of(*beyond[:2])[None])
    pieces = [kept[0], from_plane(near[1], 1), from_plane(far[0], 2), from_plane(near[0], 3)]
    scaling = 1.0 / (32.0 * tail_tokens.shape[0] * lax.axis_size("dp"))
    results = []
    for grad, noise in zip(grads, (noise_gate, noise_up, noise_down)):
        held = lax.dynamic_slice_in_dim(grad, core * rows, rows, 0)
        given = lax.dynamic_slice_in_dim(grad, (1 - core) * rows, rows, 0).astype(jnp.bfloat16)
        total = held + from_other_core(given).astype(jnp.float32)
        results.append(((total + noise[0].astype(jnp.float32)) * scaling).astype(jnp.bfloat16)[None])
    pieces, results = lax.optimization_barrier((pieces, results))
    input_grad = jnp.zeros((slice_rows, PLANES, span), jnp.bfloat16)
    for distance, piece in enumerate(pieces):
        input_grad = lax.dynamic_update_index_in_dim(input_grad, piece, (plane + distance) % PLANES, 1)
    input_grad = input_grad.reshape(1, slice_rows, D)

    return (input_grad, *results, norm_ratio)


def solution(mesh):
    weight = P("pipe", "dp", "tensor")
    in_specs = (P("pipe", "dp", None),) * 2 + (weight,) * 8 + (P("dp", None), P("dp"))
    out_specs = (P("pipe", ("dp", "tensor"), None), weight, weight, weight, P("dp"))
    return jax.shard_map(shards, mesh=mesh, in_specs=in_specs, out_specs=out_specs, check_vma=False)
```

```python
import math

import jax
import jax.numpy as jnp
from jax import lax
from jax.sharding import PartitionSpec as P

D = 2304
FF = 18432
BLOCK = 128
CORES = 2
PLANES = 4
SIDE = 4


def from_plane(value, distance):
    pairs = [
        (((plane + distance) % PLANES) * CORES + core, plane * CORES + core)
        for plane in range(PLANES)
        for core in range(CORES)
    ]
    return lax.ppermute(value, "dp", pairs)


def from_other_core(value):
    return lax.ppermute(value, "dp", [(d, d ^ 1) for d in range(PLANES * CORES)])


def along_x(value, distance):
    pairs = [
        (x * SIDE + y, ((x + distance) % SIDE) * SIDE + y) for x in range(SIDE) for y in range(SIDE)
    ]
    return lax.ppermute(value, "tensor", pairs)


def along_y(value, distance):
    pairs = [
        (x * SIDE + y, x * SIDE + (y + distance) % SIDE) for x in range(SIDE) for y in range(SIDE)
    ]
    return lax.ppermute(value, "tensor", pairs)


def paired_sum(value):
    for mask in (1, 2, 4, 8):
        value = value + lax.ppermute(value, "tensor", [(t, t ^ mask) for t in range(SIDE * SIDE)])
    return value


def block_layout(example_row, tail_local):
    quantity = tail_local.shape[0]
    member = example_row[:, None] == jnp.arange(quantity, dtype=jnp.int32)[None, :]
    following = jnp.concatenate([example_row[1:], jnp.full((1,), -1, jnp.int32)])
    closing = following != example_row
    block_tail = jnp.sum(jnp.where(member, tail_local[None, :], 0), axis=1)
    offsets = jnp.arange(BLOCK, dtype=jnp.int32)
    present = jnp.where(closing[:, None], offsets[None, :] < block_tail[:, None], True)
    return (member.astype(jnp.float32), present.reshape(-1))


def gram_matrix(matrix):
    return jnp.einsum("td,sd->ts", matrix, matrix, preferred_element_type=jnp.float32)


def example_sums(products, member):
    blocks = member.shape[0]
    span_rows = products.shape[0] // blocks
    summed = products.reshape(blocks, span_rows, blocks, span_rows).sum(axis=(1, 3))
    return jnp.sum(member * jnp.sum(summed[:, :, None] * member[None, :, :], axis=1), axis=0)


def contract(left, right):
    return jnp.einsum("tk,tj->kj", left, right, preferred_element_type=jnp.float32)


def to_neighbours(own):
    return from_plane(own, 1), from_plane(own, 3)


def to_far(after, before):
    half = after.shape[0] // 2
    return from_plane(after[:half], 1), from_plane(before[half:], 3)


def cotangents(masked, down, gate, up):
    back = jnp.dot(masked, down, preferred_element_type=jnp.float32)
    gate_f = gate.astype(jnp.float32)
    up_f = up.astype(jnp.float32)
    sigmoid_gate = jax.nn.sigmoid(gate_f)
    activated = gate_f * sigmoid_gate
    hidden = (activated * up_f).astype(jnp.bfloat16)
    up_cot = (back * activated).astype(jnp.bfloat16)
    gate_cot = (back * up_f * sigmoid_gate * (1.0 + gate_f * (1.0 - sigmoid_gate))).astype(
        jnp.bfloat16
    )
    return gate_cot, up_cot, hidden


def scatter_stage(value, place, move):
    def block(at):
        return lax.dynamic_index_in_dim(value, at % SIDE, 1, keepdims=False)

    total = block(place).astype(jnp.float32)
    for distance in (1, 2, 3):
        total = total + move(block(place + distance), distance).astype(jnp.float32)
    return total.astype(jnp.bfloat16)


def shards(
    inputs,
    out_grad,
    gate_pre,
    up_pre,
    gate_weight,
    up_weight,
    down_weight,
    noise_gate,
    noise_up,
    noise_down,
    example_of_block,
    tail_tokens,
):
    layer_in = inputs[0]
    tokens = layer_in.shape[0]
    rows = down_weight.shape[1]
    span = CORES * rows
    dp = lax.axis_index("dp")
    plane, core = dp // CORES, dp % CORES
    place = lax.axis_index("tensor")
    slice_rows = tokens // (SIDE * SIDE)

    member, present = block_layout(example_of_block[0], tail_tokens)
    masked = out_grad[0] * present.astype(jnp.bfloat16)[:, None]

    def own_span(matrix, at):
        return lax.dynamic_slice_in_dim(matrix, (at % PLANES) * span, span, 1)

    masked_piece = lax.dynamic_slice_in_dim(masked, place * slice_rows, slice_rows, 0)
    inputs_piece = lax.dynamic_slice_in_dim(layer_in, place * slice_rows, slice_rows, 0)
    received = [
        from_plane(
            jnp.concatenate([masked_piece, own_span(inputs_piece, plane - distance)], axis=1),
            distance,
        )
        for distance in (1, 2, 3)
    ]
    down_near = to_neighbours(down_weight[0])
    width = gate_pre.shape[2]
    pre_own = jnp.concatenate([gate_pre[0], up_pre[0]], axis=1)
    empty = jnp.zeros((PLANES * CORES,) + down_weight.shape[1:], jnp.bfloat16)
    across = [from_other_core(own[0]) for own in (down_weight, gate_weight, up_weight)]
    hidden_own = (jax.nn.silu(gate_pre[0].astype(jnp.float32)) * up_pre[0].astype(jnp.float32)).astype(
        jnp.bfloat16
    )
    down_products = gram_matrix(hidden_own) * gram_matrix(masked)
    received, down_near, across, pre_own, empty, gram_in, down_products = lax.optimization_barrier(
        (received, down_near, across, pre_own, empty, gram_matrix(layer_in), down_products)
    )
    down_far = to_far(*down_near)
    masked_of, inputs_of, scaled_side = [masked], [own_span(layer_in, plane)], [own_span(masked, plane)]
    received = jnp.concatenate(received, axis=0)
    received = jnp.concatenate([received, own_span(received[:, :D], plane)], axis=1)
    gathered = lax.all_gather(received, "tensor", axis=0)
    for group in range(PLANES - 1):
        whole = gathered[:, group * slice_rows : (group + 1) * slice_rows].reshape(tokens, -1)
        masked_of.append(whole[:, :D])
        inputs_of.append(whole[:, D : D + span])
        scaled_side.append(whole[:, D + span :])

    pre_own, down_far = lax.optimization_barrier((pre_own, down_far))
    pre_near = to_neighbours(pre_own)
    down_here = [down_weight[0], down_near[0], jnp.concatenate(down_far, axis=0), down_near[1]]
    down = empty
    for distance, piece in enumerate(down_here):
        at = ((plane + distance) % PLANES) * CORES
        down = lax.dynamic_update_index_in_dim(down, piece, at + core, 0)
        other = from_other_core(piece) if distance else across[0]
        down = lax.dynamic_update_index_in_dim(down, other, at + 1 - core, 0)
    down = down.reshape(D, down_weight.shape[2])

    def both_cores(own, other):
        first = core == 0
        return jnp.concatenate([jnp.where(first, own, other), jnp.where(first, other, own)], axis=0)

    gate_rows = both_cores(gate_weight[0], across[1])
    up_rows = both_cores(up_weight[0], across[2])

    gate_cot, up_cot, hidden = cotangents(masked, down, gate_pre[0], up_pre[0])
    cots = jnp.concatenate([gate_cot, up_cot], axis=1)
    products = gram_in * gram_matrix(cots) + down_products
    squares = paired_sum(example_sums(products, member))
    def scaled(matrix, factors):
        return (jnp.repeat(factors, BLOCK)[:, None] * matrix.astype(jnp.float32)).astype(jnp.bfloat16)

    def share_of(gate_cot, up_cot):
        share = jnp.einsum("tj,kj->tk", gate_cot, gate_rows, preferred_element_type=jnp.float32)
        share = share + jnp.einsum("tj,kj->tk", up_cot, up_rows, preferred_element_type=jnp.float32)
        return share.astype(jnp.bfloat16).reshape(SIDE, SIDE, slice_rows, span)

    def over_x(shares):
        return scatter_stage(shares, place // SIDE, along_x)

    def over_y(shares):
        return scatter_stage(shares, place % SIDE, along_y)

    kept = over_y(over_x(share_of(gate_cot, up_cot)[None]))
    kept, squares = lax.optimization_barrier((kept, squares))
    blocks = jnp.sum(member * squares[None, :], axis=1)
    blocks = jnp.concatenate(
        [squares, blocks] + [from_plane(blocks, distance) for distance in (1, 2, 3)]
    )
    pre_near, blocks = lax.optimization_barrier((pre_near, blocks))
    blocks = blocks + lax.ppermute(blocks, "pipe", [(0, 1), (1, 0)])
    ratios = jnp.sqrt(blocks) / (32.0 * math.sqrt(D * FF))
    examples = squares.shape[0]
    norm_ratio = ratios[:examples]
    factors = 1.0 / jnp.maximum(ratios[examples:].reshape(PLANES, -1), 1.0)
    pre_far = to_far(*pre_near)
    own = (gate_cot, up_cot, hidden)
    after = cotangents(masked_of[1], down, pre_near[0][:, :width], pre_near[0][:, width:])
    before = cotangents(masked_of[3], down, pre_near[1][:, :width], pre_near[1][:, width:])
    shares = jnp.stack([share_of(*after[:2]), share_of(*before[:2])])
    pre_far, near = lax.optimization_barrier((pre_far, over_x(shares)))
    pre_far = jnp.concatenate(pre_far, axis=0)
    beyond = cotangents(masked_of[2], down, pre_far[:, :width], pre_far[:, width:])
    far, beyond = lax.optimization_barrier((share_of(*beyond[:2])[None], beyond))
    others = over_y(jnp.concatenate([near, over_x(far)], axis=0))

    in_scaled = [scaled(inputs_of[distance], factors[distance]) for distance in range(PLANES)]
    out_scaled = [scaled(scaled_side[distance], factors[distance]) for distance in range(PLANES)]

    def grad_of(sides, index):
        near_side = jnp.concatenate([sides[0], sides[1], sides[3]], axis=0)
        near_cots = jnp.concatenate([own[index], after[index], before[index]], axis=0)
        return contract(near_side, near_cots) + contract(sides[2], beyond[index])

    grads = [grad_of(in_scaled, 0), grad_of(in_scaled, 1), grad_of(out_scaled, 2)]
    pieces = [kept[0], from_plane(others[1], 1), from_plane(others[2], 2), from_plane(others[0], 3)]
    scaling = 1.0 / (32.0 * tail_tokens.shape[0] * lax.axis_size("dp"))
    results = []
    for grad, noise in zip(grads, (noise_gate, noise_up, noise_down)):
        held = lax.dynamic_slice_in_dim(grad, core * rows, rows, 0)
        given = lax.dynamic_slice_in_dim(grad, (1 - core) * rows, rows, 0).astype(jnp.bfloat16)
        total = held + from_other_core(given).astype(jnp.float32)
        results.append(((total + noise[0].astype(jnp.float32)) * scaling).astype(jnp.bfloat16)[None])
    pieces, results = lax.optimization_barrier((pieces, results))
    input_grad = jnp.zeros((slice_rows, PLANES, span), jnp.bfloat16)
    for distance, piece in enumerate(pieces):
        input_grad = lax.dynamic_update_index_in_dim(input_grad, piece, (plane + distance) % PLANES, 1)
    input_grad = input_grad.reshape(1, slice_rows, D)

    return (input_grad, *results, norm_ratio)


def solution(mesh):
    weight = P("pipe", "dp", "tensor")
    in_specs = (P("pipe", "dp", None),) * 2 + (weight,) * 8 + (P("dp", None), P("dp"))
    out_specs = (P("pipe", ("dp", "tensor"), None), weight, weight, weight, P("dp"))
    return jax.shard_map(shards, mesh=mesh, in_specs=in_specs, out_specs=out_specs, check_vma=False)
```

```python
import math

import jax
import jax.numpy as jnp
from jax import lax
from jax.sharding import PartitionSpec as P

D = 2304
FF = 18432
BLOCK = 128
CORES = 2
PLANES = 4
SIDE = 4


def from_plane(value, distance):
    pairs = [
        (((plane + distance) % PLANES) * CORES + core, plane * CORES + core)
        for plane in range(PLANES)
        for core in range(CORES)
    ]
    return lax.ppermute(value, "dp", pairs)


def from_other_core(value):
    return lax.ppermute(value, "dp", [(d, d ^ 1) for d in range(PLANES * CORES)])


def along_x(value, distance):
    pairs = [
        (x * SIDE + y, ((x + distance) % SIDE) * SIDE + y) for x in range(SIDE) for y in range(SIDE)
    ]
    return lax.ppermute(value, "tensor", pairs)


def along_y(value, distance):
    pairs = [
        (x * SIDE + y, x * SIDE + (y + distance) % SIDE) for x in range(SIDE) for y in range(SIDE)
    ]
    return lax.ppermute(value, "tensor", pairs)


def paired_sum(value):
    for mask in (1, 2, 4, 8):
        value = value + lax.ppermute(value, "tensor", [(t, t ^ mask) for t in range(SIDE * SIDE)])
    return value


def block_layout(example_row, tail_local):
    quantity = tail_local.shape[0]
    member = example_row[:, None] == jnp.arange(quantity, dtype=jnp.int32)[None, :]
    following = jnp.concatenate([example_row[1:], jnp.full((1,), -1, jnp.int32)])
    closing = following != example_row
    block_tail = jnp.sum(jnp.where(member, tail_local[None, :], 0), axis=1)
    offsets = jnp.arange(BLOCK, dtype=jnp.int32)
    present = jnp.where(closing[:, None], offsets[None, :] < block_tail[:, None], True)
    return (member.astype(jnp.float32), present.reshape(-1))


def gram_matrix(matrix):
    return jnp.einsum("td,sd->ts", matrix, matrix, preferred_element_type=jnp.float32)


def example_sums(products, member):
    blocks = member.shape[0]
    span_rows = products.shape[0] // blocks
    summed = products.reshape(blocks, span_rows, blocks, span_rows).sum(axis=(1, 3))
    return jnp.sum(member * jnp.sum(summed[:, :, None] * member[None, :, :], axis=1), axis=0)


def contract(left, right):
    return jnp.einsum("tk,tj->kj", left, right, preferred_element_type=jnp.float32)


def to_neighbours(own):
    return from_plane(own, 1), from_plane(own, 3)


def to_far(after, before):
    half = after.shape[0] // 2
    return from_plane(after[:half], 1), from_plane(before[half:], 3)


def cotangents(masked, down, gate, up):
    back = jnp.dot(masked, down, preferred_element_type=jnp.float32)
    gate_f = gate.astype(jnp.float32)
    up_f = up.astype(jnp.float32)
    sigmoid_gate = jax.nn.sigmoid(gate_f)
    activated = gate_f * sigmoid_gate
    hidden = (activated * up_f).astype(jnp.bfloat16)
    up_cot = (back * activated).astype(jnp.bfloat16)
    gate_cot = (back * up_f * sigmoid_gate * (1.0 + gate_f * (1.0 - sigmoid_gate))).astype(
        jnp.bfloat16
    )
    return gate_cot, up_cot, hidden


def scatter_stage(value, place, move):
    def block(at):
        return lax.dynamic_index_in_dim(value, at % SIDE, 1, keepdims=False)

    total = block(place).astype(jnp.float32)
    for distance in (1, 2, 3):
        total = total + move(block(place + distance), distance).astype(jnp.float32)
    return total.astype(jnp.bfloat16)


def shards(
    inputs,
    out_grad,
    gate_pre,
    up_pre,
    gate_weight,
    up_weight,
    down_weight,
    noise_gate,
    noise_up,
    noise_down,
    example_of_block,
    tail_tokens,
):
    layer_in = inputs[0]
    tokens = layer_in.shape[0]
    rows = down_weight.shape[1]
    span = CORES * rows
    dp = lax.axis_index("dp")
    plane, core = dp // CORES, dp % CORES
    place = lax.axis_index("tensor")
    slice_rows = tokens // (SIDE * SIDE)

    member, present = block_layout(example_of_block[0], tail_tokens)
    masked = out_grad[0] * present.astype(jnp.bfloat16)[:, None]

    def own_span(matrix, at):
        return lax.dynamic_slice_in_dim(matrix, (at % PLANES) * span, span, 1)

    masked_piece = lax.dynamic_slice_in_dim(masked, place * slice_rows, slice_rows, 0)
    inputs_piece = lax.dynamic_slice_in_dim(layer_in, place * slice_rows, slice_rows, 0)
    received = [
        from_plane(
            jnp.concatenate([masked_piece, own_span(inputs_piece, plane - distance)], axis=1),
            distance,
        )
        for distance in (1, 2, 3)
    ]
    down_near = to_neighbours(down_weight[0])
    width = gate_pre.shape[2]
    pre_own = jnp.concatenate([gate_pre[0], up_pre[0]], axis=1)
    empty = jnp.zeros((PLANES * CORES,) + down_weight.shape[1:], jnp.bfloat16)
    received, weights = lax.optimization_barrier(
        (received, (down_weight[0], gate_weight[0], up_weight[0]))
    )
    across = [from_other_core(weight) for weight in weights]
    hidden_own = (jax.nn.silu(gate_pre[0].astype(jnp.float32)) * up_pre[0].astype(jnp.float32)).astype(
        jnp.bfloat16
    )
    down_products = gram_matrix(hidden_own) * gram_matrix(masked)
    received, down_near, across, pre_own, empty, gram_in, down_products = lax.optimization_barrier(
        (received, down_near, across, pre_own, empty, gram_matrix(layer_in), down_products)
    )
    down_far = to_far(*down_near)
    masked_of, inputs_of, scaled_side = [masked], [own_span(layer_in, plane)], [own_span(masked, plane)]
    received = jnp.concatenate(received, axis=0)
    received = jnp.concatenate([received, own_span(received[:, :D], plane)], axis=1)
    gathered = lax.all_gather(received, "tensor", axis=0)
    for group in range(PLANES - 1):
        whole = gathered[:, group * slice_rows : (group + 1) * slice_rows].reshape(tokens, -1)
        masked_of.append(whole[:, :D])
        inputs_of.append(whole[:, D : D + span])
        scaled_side.append(whole[:, D + span :])

    pre_own, down_far = lax.optimization_barrier((pre_own, down_far))
    pre_near = to_neighbours(pre_own)
    down_here = [down_weight[0], down_near[0], jnp.concatenate(down_far, axis=0), down_near[1]]
    down = empty
    for distance, piece in enumerate(down_here):
        at = ((plane + distance) % PLANES) * CORES
        down = lax.dynamic_update_index_in_dim(down, piece, at + core, 0)
        other = from_other_core(piece) if distance else across[0]
        down = lax.dynamic_update_index_in_dim(down, other, at + 1 - core, 0)
    down = down.reshape(D, down_weight.shape[2])

    def both_cores(own, other):
        first = core == 0
        return jnp.concatenate([jnp.where(first, own, other), jnp.where(first, other, own)], axis=0)

    gate_rows = both_cores(gate_weight[0], across[1])
    up_rows = both_cores(up_weight[0], across[2])

    gate_cot, up_cot, hidden = cotangents(masked, down, gate_pre[0], up_pre[0])
    cots = jnp.concatenate([gate_cot, up_cot], axis=1)
    products = gram_in * gram_matrix(cots) + down_products
    squares = paired_sum(example_sums(products, member))
    def scaled(matrix, factors):
        return (jnp.repeat(factors, BLOCK)[:, None] * matrix.astype(jnp.float32)).astype(jnp.bfloat16)

    def share_of(gate_cot, up_cot):
        share = jnp.einsum("tj,kj->tk", gate_cot, gate_rows, preferred_element_type=jnp.float32)
        share = share + jnp.einsum("tj,kj->tk", up_cot, up_rows, preferred_element_type=jnp.float32)
        return share.astype(jnp.bfloat16).reshape(SIDE, SIDE, slice_rows, span)

    def over_x(shares):
        return scatter_stage(shares, place // SIDE, along_x)

    def over_y(shares):
        return scatter_stage(shares, place % SIDE, along_y)

    kept = over_y(over_x(share_of(gate_cot, up_cot)[None]))
    kept, squares = lax.optimization_barrier((kept, squares))
    blocks = jnp.sum(member * squares[None, :], axis=1)
    blocks = jnp.concatenate(
        [squares, blocks] + [from_plane(blocks, distance) for distance in (1, 2, 3)]
    )
    pre_near, blocks = lax.optimization_barrier((pre_near, blocks))
    blocks = blocks + lax.ppermute(blocks, "pipe", [(0, 1), (1, 0)])
    ratios = jnp.sqrt(blocks) / (32.0 * math.sqrt(D * FF))
    examples = squares.shape[0]
    norm_ratio = ratios[:examples]
    factors = 1.0 / jnp.maximum(ratios[examples:].reshape(PLANES, -1), 1.0)
    pre_far = to_far(*pre_near)
    own = (gate_cot, up_cot, hidden)
    after = cotangents(masked_of[1], down, pre_near[0][:, :width], pre_near[0][:, width:])
    before = cotangents(masked_of[3], down, pre_near[1][:, :width], pre_near[1][:, width:])
    near = [over_x(share_of(*cots[:2])[None]) for cots in (after, before)]
    pre_far, near = lax.optimization_barrier((pre_far, near))
    pre_far = jnp.concatenate(pre_far, axis=0)
    far = cotangents(masked_of[2], down, pre_far[:, :width], pre_far[:, width:])
    share, groups = lax.optimization_barrier((share_of(*far[:2])[None], (own, after, far, before)))
    others = over_y(jnp.concatenate(near + [over_x(share)], axis=0))

    in_scaled = [scaled(inputs_of[distance], factors[distance]) for distance in range(PLANES)]
    out_scaled = [scaled(scaled_side[distance], factors[distance]) for distance in range(PLANES)]

    def grad_of(sides, index):
        cots = jnp.concatenate([group[index] for group in groups], axis=0)
        return contract(jnp.concatenate(sides, axis=0), cots)

    grads = [grad_of(in_scaled, 0), grad_of(in_scaled, 1), grad_of(out_scaled, 2)]
    pieces = [kept[0], from_plane(others[1], 1), from_plane(others[2], 2), from_plane(others[0], 3)]
    scaling = 1.0 / (32.0 * tail_tokens.shape[0] * lax.axis_size("dp"))
    results = []
    for grad, noise in zip(grads, (noise_gate, noise_up, noise_down)):
        held = lax.dynamic_slice_in_dim(grad, core * rows, rows, 0)
        given = lax.dynamic_slice_in_dim(grad, (1 - core) * rows, rows, 0).astype(jnp.bfloat16)
        total = held + from_other_core(given).astype(jnp.float32)
        results.append(((total + noise[0].astype(jnp.float32)) * scaling).astype(jnp.bfloat16)[None])
    pieces, results = lax.optimization_barrier((pieces, results))
    input_grad = jnp.zeros((slice_rows, PLANES, span), jnp.bfloat16)
    for distance, piece in enumerate(pieces):
        input_grad = lax.dynamic_update_index_in_dim(input_grad, piece, (plane + distance) % PLANES, 1)
    input_grad = input_grad.reshape(1, slice_rows, D)

    return (input_grad, *results, norm_ratio)


def solution(mesh):
    weight = P("pipe", "dp", "tensor")
    in_specs = (P("pipe", "dp", None),) * 2 + (weight,) * 8 + (P("dp", None), P("dp"))
    out_specs = (P("pipe", ("dp", "tensor"), None), weight, weight, weight, P("dp"))
    return jax.shard_map(shards, mesh=mesh, in_specs=in_specs, out_specs=out_specs, check_vma=False)
```

```python
import math

import jax
import jax.numpy as jnp
from jax import lax
from jax.sharding import PartitionSpec as P

D = 2304
FF = 18432
BLOCK = 128
CORES = 2
PLANES = 4
SIDE = 4


def from_plane(value, distance):
    pairs = [
        (((plane + distance) % PLANES) * CORES + core, plane * CORES + core)
        for plane in range(PLANES)
        for core in range(CORES)
    ]
    return lax.ppermute(value, "dp", pairs)


def from_other_core(value):
    return lax.ppermute(value, "dp", [(d, d ^ 1) for d in range(PLANES * CORES)])


def along_x(value, distance):
    pairs = [
        (x * SIDE + y, ((x + distance) % SIDE) * SIDE + y) for x in range(SIDE) for y in range(SIDE)
    ]
    return lax.ppermute(value, "tensor", pairs)


def along_y(value, distance):
    pairs = [
        (x * SIDE + y, x * SIDE + (y + distance) % SIDE) for x in range(SIDE) for y in range(SIDE)
    ]
    return lax.ppermute(value, "tensor", pairs)


def paired_sum(value):
    for mask in (1, 2, 4, 8):
        value = value + lax.ppermute(value, "tensor", [(t, t ^ mask) for t in range(SIDE * SIDE)])
    return value


def block_layout(example_row, tail_local):
    quantity = tail_local.shape[0]
    member = example_row[:, None] == jnp.arange(quantity, dtype=jnp.int32)[None, :]
    following = jnp.concatenate([example_row[1:], jnp.full((1,), -1, jnp.int32)])
    closing = following != example_row
    block_tail = jnp.sum(jnp.where(member, tail_local[None, :], 0), axis=1)
    offsets = jnp.arange(BLOCK, dtype=jnp.int32)
    present = jnp.where(closing[:, None], offsets[None, :] < block_tail[:, None], True)
    return (member.astype(jnp.float32), present.reshape(-1))


def gram_matrix(matrix):
    return jnp.einsum("td,sd->ts", matrix, matrix, preferred_element_type=jnp.float32)


def example_sums(products, member):
    blocks = member.shape[0]
    span_rows = products.shape[0] // blocks
    summed = products.reshape(blocks, span_rows, blocks, span_rows).sum(axis=(1, 3))
    return jnp.sum(member * jnp.sum(summed[:, :, None] * member[None, :, :], axis=1), axis=0)


def contract(left, right):
    return jnp.einsum("tk,tj->kj", left, right, preferred_element_type=jnp.float32)


def to_neighbours(own):
    return from_plane(own, 1), from_plane(own, 3)


def to_far(after, before):
    half = after.shape[0] // 2
    return from_plane(after[:half], 1), from_plane(before[half:], 3)


def cotangents(masked, down, gate, up):
    back = jnp.dot(masked, down, preferred_element_type=jnp.float32)
    gate_f = gate.astype(jnp.float32)
    up_f = up.astype(jnp.float32)
    sigmoid_gate = jax.nn.sigmoid(gate_f)
    activated = gate_f * sigmoid_gate
    hidden = (activated * up_f).astype(jnp.bfloat16)
    up_cot = (back * activated).astype(jnp.bfloat16)
    gate_cot = (back * up_f * sigmoid_gate * (1.0 + gate_f * (1.0 - sigmoid_gate))).astype(
        jnp.bfloat16
    )
    return gate_cot, up_cot, hidden


def blocks_of(value, place):
    return [
        lax.dynamic_index_in_dim(value, (place + distance) % SIDE, 1, keepdims=False)
        for distance in range(SIDE)
    ]


def sum_blocks(blocks, move):
    total = blocks[0].astype(jnp.float32)
    for distance in (1, 2, 3):
        total = total + move(blocks[distance], distance).astype(jnp.float32)
    return total.astype(jnp.bfloat16)


def shards(
    inputs,
    out_grad,
    gate_pre,
    up_pre,
    gate_weight,
    up_weight,
    down_weight,
    noise_gate,
    noise_up,
    noise_down,
    example_of_block,
    tail_tokens,
):
    layer_in = inputs[0]
    tokens = layer_in.shape[0]
    rows = down_weight.shape[1]
    span = CORES * rows
    dp = lax.axis_index("dp")
    plane, core = dp // CORES, dp % CORES
    place = lax.axis_index("tensor")
    slice_rows = tokens // (SIDE * SIDE)

    member, present = block_layout(example_of_block[0], tail_tokens)
    masked = out_grad[0] * present.astype(jnp.bfloat16)[:, None]

    def own_span(matrix, at):
        return lax.dynamic_slice_in_dim(matrix, (at % PLANES) * span, span, 1)

    masked_piece = lax.dynamic_slice_in_dim(masked, place * slice_rows, slice_rows, 0)
    inputs_piece = lax.dynamic_slice_in_dim(layer_in, place * slice_rows, slice_rows, 0)
    received = [
        from_plane(
            jnp.concatenate([masked_piece, own_span(inputs_piece, plane - distance)], axis=1),
            distance,
        )
        for distance in (1, 2, 3)
    ]
    down_near = to_neighbours(down_weight[0])
    width = gate_pre.shape[2]
    pre_own = jnp.concatenate([gate_pre[0], up_pre[0]], axis=1)
    empty = jnp.zeros((PLANES * CORES,) + down_weight.shape[1:], jnp.bfloat16)
    received, weights = lax.optimization_barrier(
        (received, (down_weight[0], gate_weight[0], up_weight[0]))
    )
    across = [from_other_core(weight) for weight in weights]
    hidden_own = (jax.nn.silu(gate_pre[0].astype(jnp.float32)) * up_pre[0].astype(jnp.float32)).astype(
        jnp.bfloat16
    )
    down_products = gram_matrix(hidden_own) * gram_matrix(masked)
    received, down_near, across, pre_own, empty, gram_in, down_products = lax.optimization_barrier(
        (received, down_near, across, pre_own, empty, gram_matrix(layer_in), down_products)
    )
    down_far = to_far(*down_near)
    masked_of, inputs_of, scaled_side = [masked], [own_span(layer_in, plane)], [own_span(masked, plane)]
    received = jnp.concatenate(received, axis=0)
    received = jnp.concatenate([received, own_span(received[:, :D], plane)], axis=1)
    gathered = lax.all_gather(received, "tensor", axis=0)
    whole = [
        gathered[:, group * slice_rows : (group + 1) * slice_rows].reshape(tokens, -1)
        for group in range(PLANES - 1)
    ]

    pre_own, down_far = lax.optimization_barrier((pre_own, down_far))
    pre_near = to_neighbours(pre_own)
    down_here = [down_weight[0], down_near[0], jnp.concatenate(down_far, axis=0), down_near[1]]
    down = empty
    for distance, piece in enumerate(down_here):
        at = ((plane + distance) % PLANES) * CORES
        down = lax.dynamic_update_index_in_dim(down, piece, at + core, 0)
        other = from_other_core(piece) if distance else across[0]
        down = lax.dynamic_update_index_in_dim(down, other, at + 1 - core, 0)
    down = down.reshape(D, down_weight.shape[2])

    def both_cores(own, other):
        first = core == 0
        return jnp.concatenate([jnp.where(first, own, other), jnp.where(first, other, own)], axis=0)

    gate_rows = both_cores(gate_weight[0], across[1])
    up_rows = both_cores(up_weight[0], across[2])

    gate_cot, up_cot, hidden = cotangents(masked, down, gate_pre[0], up_pre[0])
    cots = jnp.concatenate([gate_cot, up_cot], axis=1)
    products = gram_in * gram_matrix(cots) + down_products
    squares = paired_sum(example_sums(products, member))
    def scaled(matrix, factors):
        return (jnp.repeat(factors, BLOCK)[:, None] * matrix.astype(jnp.float32)).astype(jnp.bfloat16)

    def share_of(gate_cot, up_cot):
        share = jnp.einsum("tj,kj->tk", gate_cot, gate_rows, preferred_element_type=jnp.float32)
        share = share + jnp.einsum("tj,kj->tk", up_cot, up_rows, preferred_element_type=jnp.float32)
        return share.astype(jnp.bfloat16).reshape(SIDE, SIDE, slice_rows, span)

    def over_x(shares):
        return sum_blocks(blocks_of(shares, place // SIDE), along_x)

    def over_y(shares):
        return sum_blocks(blocks_of(shares, place % SIDE), along_y)

    kept = over_y(over_x(share_of(gate_cot, up_cot)[None]))
    kept, squares = lax.optimization_barrier((kept, squares))
    blocks = jnp.sum(member * squares[None, :], axis=1)
    blocks = jnp.concatenate(
        [squares, blocks] + [from_plane(blocks, distance) for distance in (1, 2, 3)]
    )
    pre_near, blocks, whole = lax.optimization_barrier((pre_near, blocks, whole))
    for rows_of in whole:
        masked_of.append(rows_of[:, :D])
        inputs_of.append(rows_of[:, D : D + span])
        scaled_side.append(rows_of[:, D + span :])
    blocks = blocks + lax.ppermute(blocks, "pipe", [(0, 1), (1, 0)])
    ratios = jnp.sqrt(blocks) / (32.0 * math.sqrt(D * FF))
    examples = squares.shape[0]
    norm_ratio = ratios[:examples]
    factors = 1.0 / jnp.maximum(ratios[examples:].reshape(PLANES, -1), 1.0)
    pre_far = to_far(*pre_near)
    pre_near, factors = lax.optimization_barrier((pre_near, factors))
    own = (gate_cot, up_cot, hidden)
    after = cotangents(masked_of[1], down, pre_near[0][:, :width], pre_near[0][:, width:])
    before = cotangents(masked_of[3], down, pre_near[1][:, :width], pre_near[1][:, width:])
    in_scaled = [scaled(inputs_of[distance], factors[distance]) for distance in range(PLANES)]
    out_scaled = [scaled(scaled_side[distance], factors[distance]) for distance in range(PLANES)]
    before_blocks = blocks_of(share_of(*before[:2])[None], place // SIDE)
    after_sum = over_x(share_of(*after[:2])[None])
    pre_far, after_sum, before_blocks, in_scaled, out_scaled = lax.optimization_barrier(
        (pre_far, after_sum, before_blocks, in_scaled, out_scaled)
    )
    pre_far = jnp.concatenate(pre_far, axis=0)
    far = cotangents(masked_of[2], down, pre_far[:, :width], pre_far[:, width:])
    far_blocks = blocks_of(share_of(*far[:2])[None], place // SIDE)
    two = [jnp.concatenate(pair, axis=0) for pair in zip(far_blocks, before_blocks)]
    two, groups = lax.optimization_barrier((two, (own, after, far, before)))
    two_sum = sum_blocks(two, along_x)
    others = over_y(jnp.concatenate([after_sum, two_sum], axis=0))

    def grad_of(sides, index):
        cots = jnp.concatenate([group[index] for group in groups], axis=0)
        return contract(jnp.concatenate(sides, axis=0), cots)

    grads = [grad_of(in_scaled, 0), grad_of(in_scaled, 1), grad_of(out_scaled, 2)]
    pieces = [kept[0], from_plane(others[2], 1), from_plane(others[1], 2), from_plane(others[0], 3)]
    scaling = 1.0 / (32.0 * tail_tokens.shape[0] * lax.axis_size("dp"))
    results = []
    for grad, noise in zip(grads, (noise_gate, noise_up, noise_down)):
        held = lax.dynamic_slice_in_dim(grad, core * rows, rows, 0)
        given = lax.dynamic_slice_in_dim(grad, (1 - core) * rows, rows, 0).astype(jnp.bfloat16)
        total = held + from_other_core(given).astype(jnp.float32)
        results.append(((total + noise[0].astype(jnp.float32)) * scaling).astype(jnp.bfloat16)[None])
    pieces, results = lax.optimization_barrier((pieces, results))
    stacked = jnp.stack(pieces)
    input_grad = jnp.concatenate(
        [
            lax.dynamic_index_in_dim(stacked, (at - plane) % PLANES, 0, keepdims=False)
            for at in range(PLANES)
        ],
        axis=1,
    )[None]
    return (input_grad, *results, norm_ratio)


def solution(mesh):
    weight = P("pipe", "dp", "tensor")
    in_specs = (P("pipe", "dp", None),) * 2 + (weight,) * 8 + (P("dp", None), P("dp"))
    out_specs = (P("pipe", ("dp", "tensor"), None), weight, weight, weight, P("dp"))
    return jax.shard_map(shards, mesh=mesh, in_specs=in_specs, out_specs=out_specs, check_vma=False)
```

```python
import math

import jax
import jax.numpy as jnp
from jax import lax
from jax.sharding import PartitionSpec as P

D = 2304
FF = 18432
BLOCK = 128
CORES = 2
PLANES = 4
SIDE = 4


def from_plane(value, distance):
    pairs = [
        (((plane + distance) % PLANES) * CORES + core, plane * CORES + core)
        for plane in range(PLANES)
        for core in range(CORES)
    ]
    return lax.ppermute(value, "dp", pairs)


def from_other_core(value):
    return lax.ppermute(value, "dp", [(d, d ^ 1) for d in range(PLANES * CORES)])


def along_x(value, distance):
    pairs = [
        (x * SIDE + y, ((x + distance) % SIDE) * SIDE + y) for x in range(SIDE) for y in range(SIDE)
    ]
    return lax.ppermute(value, "tensor", pairs)


def along_y(value, distance):
    pairs = [
        (x * SIDE + y, x * SIDE + (y + distance) % SIDE) for x in range(SIDE) for y in range(SIDE)
    ]
    return lax.ppermute(value, "tensor", pairs)


def paired_sum(value):
    for mask in (1, 2, 4, 8):
        value = value + lax.ppermute(value, "tensor", [(t, t ^ mask) for t in range(SIDE * SIDE)])
    return value


def block_layout(example_row, tail_local):
    quantity = tail_local.shape[0]
    member = example_row[:, None] == jnp.arange(quantity, dtype=jnp.int32)[None, :]
    following = jnp.concatenate([example_row[1:], jnp.full((1,), -1, jnp.int32)])
    closing = following != example_row
    block_tail = jnp.sum(jnp.where(member, tail_local[None, :], 0), axis=1)
    offsets = jnp.arange(BLOCK, dtype=jnp.int32)
    present = jnp.where(closing[:, None], offsets[None, :] < block_tail[:, None], True)
    return (member.astype(jnp.float32), present.reshape(-1))


def gram_matrix(matrix):
    return jnp.einsum("td,sd->ts", matrix, matrix, preferred_element_type=jnp.float32)


def example_sums(products, member):
    blocks = member.shape[0]
    span_rows = products.shape[0] // blocks
    summed = products.reshape(blocks, span_rows, blocks, span_rows).sum(axis=(1, 3))
    return jnp.sum(member * jnp.sum(summed[:, :, None] * member[None, :, :], axis=1), axis=0)


def contract(left, right):
    return jnp.einsum("tk,tj->kj", left, right, preferred_element_type=jnp.float32)


def to_neighbours(own):
    return from_plane(own, 1), from_plane(own, 3)


def to_far(after, before):
    half = after.shape[0] // 2
    return from_plane(after[:half], 1), from_plane(before[half:], 3)


def cotangents(masked, down, gate, up):
    back = jnp.dot(masked, down, preferred_element_type=jnp.float32)
    gate_f = gate.astype(jnp.float32)
    up_f = up.astype(jnp.float32)
    sigmoid_gate = jax.nn.sigmoid(gate_f)
    activated = gate_f * sigmoid_gate
    hidden = (activated * up_f).astype(jnp.bfloat16)
    up_cot = (back * activated).astype(jnp.bfloat16)
    gate_cot = (back * up_f * sigmoid_gate * (1.0 + gate_f * (1.0 - sigmoid_gate))).astype(
        jnp.bfloat16
    )
    return gate_cot, up_cot, hidden


def blocks_of(value, place):
    return [
        lax.dynamic_index_in_dim(value, (place + distance) % SIDE, 1, keepdims=False)
        for distance in range(SIDE)
    ]


def sum_blocks(blocks, move):
    total = blocks[0].astype(jnp.float32)
    for distance in (1, 2, 3):
        total = total + move(blocks[distance], distance).astype(jnp.float32)
    return total.astype(jnp.bfloat16)


def shards(
    inputs,
    out_grad,
    gate_pre,
    up_pre,
    gate_weight,
    up_weight,
    down_weight,
    noise_gate,
    noise_up,
    noise_down,
    example_of_block,
    tail_tokens,
):
    layer_in = inputs[0]
    tokens = layer_in.shape[0]
    rows = down_weight.shape[1]
    span = CORES * rows
    dp = lax.axis_index("dp")
    plane, core = dp // CORES, dp % CORES
    place = lax.axis_index("tensor")
    slice_rows = tokens // (SIDE * SIDE)

    member, present = block_layout(example_of_block[0], tail_tokens)
    masked = out_grad[0] * present.astype(jnp.bfloat16)[:, None]

    def own_span(matrix, at):
        return lax.dynamic_slice_in_dim(matrix, (at % PLANES) * span, span, 1)

    masked_piece = lax.dynamic_slice_in_dim(masked, place * slice_rows, slice_rows, 0)
    inputs_piece = lax.dynamic_slice_in_dim(layer_in, place * slice_rows, slice_rows, 0)
    received = [
        from_plane(
            jnp.concatenate([masked_piece, own_span(inputs_piece, plane - distance)], axis=1),
            distance,
        )
        for distance in (1, 2, 3)
    ]
    down_near = to_neighbours(down_weight[0])
    width = gate_pre.shape[2]
    pre_own = jnp.concatenate([gate_pre[0], up_pre[0]], axis=1)
    empty = jnp.zeros((PLANES * CORES,) + down_weight.shape[1:], jnp.bfloat16)
    received, weights = lax.optimization_barrier(
        (received, (down_weight[0], gate_weight[0], up_weight[0]))
    )
    across = [from_other_core(weight) for weight in weights]
    hidden_own = (jax.nn.silu(gate_pre[0].astype(jnp.float32)) * up_pre[0].astype(jnp.float32)).astype(
        jnp.bfloat16
    )
    down_products = gram_matrix(hidden_own) * gram_matrix(masked)
    received, down_near, across, pre_own, empty, gram_in, down_products = lax.optimization_barrier(
        (received, down_near, across, pre_own, empty, gram_matrix(layer_in), down_products)
    )
    down_far = to_far(*down_near)
    masked_of, inputs_of, scaled_side = [masked], [own_span(layer_in, plane)], [own_span(masked, plane)]
    received = jnp.concatenate(received, axis=0)
    received = jnp.concatenate([received, own_span(received[:, :D], plane)], axis=1)
    gathered = lax.all_gather(received, "tensor", axis=0)
    whole = [
        gathered[:, group * slice_rows : (group + 1) * slice_rows].reshape(tokens, -1)
        for group in range(PLANES - 1)
    ]

    pre_own, down_far = lax.optimization_barrier((pre_own, down_far))
    pre_near = to_neighbours(pre_own)
    down_here = [down_weight[0], down_near[0], jnp.concatenate(down_far, axis=0), down_near[1]]
    down = empty
    for distance, piece in enumerate(down_here):
        at = ((plane + distance) % PLANES) * CORES
        down = lax.dynamic_update_index_in_dim(down, piece, at + core, 0)
        other = from_other_core(piece) if distance else across[0]
        down = lax.dynamic_update_index_in_dim(down, other, at + 1 - core, 0)
    down = down.reshape(D, down_weight.shape[2])

    def both_cores(own, other):
        first = core == 0
        return jnp.concatenate([jnp.where(first, own, other), jnp.where(first, other, own)], axis=0)

    gate_rows = both_cores(gate_weight[0], across[1])
    up_rows = both_cores(up_weight[0], across[2])

    gate_cot, up_cot, hidden = cotangents(masked, down, gate_pre[0], up_pre[0])
    cots = jnp.concatenate([gate_cot, up_cot], axis=1)
    products = gram_in * gram_matrix(cots) + down_products
    squares = paired_sum(example_sums(products, member))
    def scaled(matrix, factors):
        return (jnp.repeat(factors, BLOCK)[:, None] * matrix.astype(jnp.float32)).astype(jnp.bfloat16)

    def share_of(gate_cot, up_cot):
        share = jnp.einsum("tj,kj->tk", gate_cot, gate_rows, preferred_element_type=jnp.float32)
        share = share + jnp.einsum("tj,kj->tk", up_cot, up_rows, preferred_element_type=jnp.float32)
        return share.astype(jnp.bfloat16).reshape(SIDE, SIDE, slice_rows, span)

    def over_x(shares):
        return sum_blocks(blocks_of(shares, place // SIDE), along_x)

    def over_y(shares):
        return sum_blocks(blocks_of(shares, place % SIDE), along_y)

    kept = over_y(over_x(share_of(gate_cot, up_cot)[None]))
    kept, squares = lax.optimization_barrier((kept, squares))
    blocks = jnp.sum(member * squares[None, :], axis=1)
    blocks = jnp.concatenate(
        [squares, blocks] + [from_plane(blocks, distance) for distance in (1, 2, 3)]
    )
    pre_near, blocks = lax.optimization_barrier((pre_near, blocks))
    for rows_of in whole:
        masked_of.append(rows_of[:, :D])
        inputs_of.append(rows_of[:, D : D + span])
        scaled_side.append(rows_of[:, D + span :])
    blocks = blocks + lax.ppermute(blocks, "pipe", [(0, 1), (1, 0)])
    ratios = jnp.sqrt(blocks) / (32.0 * math.sqrt(D * FF))
    examples = squares.shape[0]
    norm_ratio = ratios[:examples]
    factors = 1.0 / jnp.maximum(ratios[examples:].reshape(PLANES, -1), 1.0)
    pre_far = to_far(*pre_near)
    pre_near, factors = lax.optimization_barrier((pre_near, factors))
    own = (gate_cot, up_cot, hidden)
    after = cotangents(masked_of[1], down, pre_near[0][:, :width], pre_near[0][:, width:])
    before = cotangents(masked_of[3], down, pre_near[1][:, :width], pre_near[1][:, width:])
    in_scaled = [scaled(inputs_of[distance], factors[distance]) for distance in range(PLANES)]
    out_scaled = [scaled(scaled_side[distance], factors[distance]) for distance in range(PLANES)]
    before_blocks = blocks_of(share_of(*before[:2])[None], place // SIDE)
    after_sum = over_x(share_of(*after[:2])[None])
    pre_far, after_sum, before_blocks, in_scaled, out_scaled = lax.optimization_barrier(
        (pre_far, after_sum, before_blocks, in_scaled, out_scaled)
    )
    pre_far = jnp.concatenate(pre_far, axis=0)
    far = cotangents(masked_of[2], down, pre_far[:, :width], pre_far[:, width:])
    far_blocks = blocks_of(share_of(*far[:2])[None], place // SIDE)
    two = [jnp.concatenate(pair, axis=0) for pair in zip(far_blocks, before_blocks)]
    two, groups = lax.optimization_barrier((two, (own, after, far, before)))
    two_sum = sum_blocks(two, along_x)
    others = over_y(jnp.concatenate([after_sum, two_sum], axis=0))

    def grad_of(sides, index):
        cots = jnp.concatenate([group[index] for group in groups], axis=0)
        return contract(jnp.concatenate(sides, axis=0), cots)

    grads = [grad_of(in_scaled, 0), grad_of(in_scaled, 1), grad_of(out_scaled, 2)]
    pieces = [kept[0], from_plane(others[2], 1), from_plane(others[1], 2), from_plane(others[0], 3)]
    scaling = 1.0 / (32.0 * tail_tokens.shape[0] * lax.axis_size("dp"))
    results = []
    for grad, noise in zip(grads, (noise_gate, noise_up, noise_down)):
        held = lax.dynamic_slice_in_dim(grad, core * rows, rows, 0)
        given = lax.dynamic_slice_in_dim(grad, (1 - core) * rows, rows, 0).astype(jnp.bfloat16)
        total = held + from_other_core(given).astype(jnp.float32)
        results.append(((total + noise[0].astype(jnp.float32)) * scaling).astype(jnp.bfloat16)[None])
    pieces, results = lax.optimization_barrier((pieces, results))
    stacked = jnp.stack(pieces)
    input_grad = jnp.concatenate(
        [
            lax.dynamic_index_in_dim(stacked, (at - plane) % PLANES, 0, keepdims=False)
            for at in range(PLANES)
        ],
        axis=1,
    )[None]
    return (input_grad, *results, norm_ratio)


def solution(mesh):
    weight = P("pipe", "dp", "tensor")
    in_specs = (P("pipe", "dp", None),) * 2 + (weight,) * 8 + (P("dp", None), P("dp"))
    out_specs = (P("pipe", ("dp", "tensor"), None), weight, weight, weight, P("dp"))
    return jax.shard_map(shards, mesh=mesh, in_specs=in_specs, out_specs=out_specs, check_vma=False)
```
